32 devices in a mesh: wide: 8 (over z, core), narrow: 4 (over y, x).
Axes of the slice: x: 2, y: 2, z: 4, core: 2. Of those that a mesh axis runs over, the one named last changes fastest.
Arguments:
- source: float32 [128, 512, 128], P('wide', 'narrow'), may hold values from -14 to 14, as said below
- reaction: float32 [128, 512, 128], P('wide', 'narrow'), may hold values from 0.02 to 0.2
- conductance: float32 [128, 512, 128], P('wide', 'narrow'), may hold values from 0.25 to 2
- coarse_inverse: float32 [8, 4, 8, 256], P('wide', 'narrow'), may hold values from -1 to 16, as said below
Outputs:
- solution: float32 [128, 512, 128], P('wide', 'narrow')
- residual: float32 [128, 512, 128], P('wide', 'narrow')
- direction: float32 [128, 512, 128], P('wide', 'narrow')
The draws below stay inside these ranges and needn't reach their ends.
Inputs may be any that keep to these rules, and one draw needn't show every extreme that they name: source: finite values of either sign. coarse_inverse: a symmetric positive definite matrix.
All inputs are finite; a program needn't handle non-finite values.
Results may differ from the reference program's by a relative error of at most 0.0003.
Values sent between devices are 32-bit elements; how exact they have to be, the bound alone decides.
A program may use at most 64 MiB of HBM per device.

```python
import math
import jax
import jax.numpy as jnp
from jax import lax

CX = 16
CY = 128
CZ = 128
W = 8
PRIMAL = 8
ITERS = 2
NX = 128
NY = 512
NZ = 128
SUBS_W = 8
SUBS_N = 4
COARSE = 256
N_WIDE = 8
N_NARROW = 4


def draw_source(key, part):
    key_rough, key_phase = jax.random.split(key)
    place_x = jnp.arange(NX, dtype=jnp.float32)[:, None, None] / NX
    place_y = jnp.arange(NY, dtype=jnp.float32)[None, :, None] / NY
    place_z = jnp.arange(NZ, dtype=jnp.float32)[None, None, :] / NZ
    phases = jax.random.uniform(key_phase, (3,), jnp.float32, 0.0, 6.283)
    smooth = 0.6 * jnp.sin(18.85 * place_x + phases[0]) * jnp.cos(12.566 * place_y + phases[1]) * jnp.cos(3.1416 * place_z + phases[2])
    ramp = 1.0 + 2.0 * place_x
    rough = jnp.clip(jax.random.normal(key_rough, (NX, NY, NZ), jnp.float32), -4.0, 4.0)
    return (ramp * (rough + smooth)).astype(jnp.float32)


def draw_coarse_inverse(key, part):
    key_diag, key_off = jax.random.split(key)
    diagonal = jnp.exp(jax.random.uniform(key_diag, (COARSE,), jnp.float32, 1.3863, 2.7725))
    uniform_raw = jax.random.uniform(key_off, (COARSE, COARSE), jnp.float32, -1.0, 1.0)
    symmetric = 0.5 * (uniform_raw + uniform_raw.T)
    scaling = jnp.sqrt(diagonal[:, None] * diagonal[None, :])
    off_scale = 0.5 / float(COARSE) ** 0.5
    identity_mask = jnp.arange(COARSE)[:, None] == jnp.arange(COARSE)[None, :]
    matrix = jnp.where(identity_mask, diagonal[:, None] * jnp.ones((1, COARSE), jnp.float32), off_scale * symmetric * scaling)
    return matrix.reshape(SUBS_W, SUBS_N, PRIMAL, COARSE).astype(jnp.float32)


def level_of(own_key, shape, pieces, smallest, high):
    factor_of = 1.0
    for dim, blocks in pieces:
        steps = jax.random.uniform(jax.random.fold_in(jax.random.fold_in(own_key, 6), dim), (blocks,), jnp.float32, smallest / len(pieces), high / len(pieces))
        factor_of = factor_of * jnp.repeat(jnp.exp(steps), shape[dim] // blocks).reshape((-1,) + (1,) * (len(shape) - 1 - dim))
    return factor_of


def setup_inputs(seed: int = 0) -> dict:
    seeds = jax.random.split(jax.random.key(seed), 5)
    source = draw_source(jax.random.fold_in(seeds[4], 71), 0)
    reaction = jnp.clip(jnp.exp(math.log(0.2) - 2.3025851 * jax.random.uniform(seeds[1], (NX, NY, NZ), jnp.float32) ** level_of(seeds[1], (NX, NY, NZ), ((0, 8), (1, 4)), -0.2, 0.2)), 0.02, 0.2)
    conductance = jnp.clip(jnp.exp(math.log(2.0) - 2.0794415 * jax.random.uniform(seeds[2], (NX, NY, NZ), jnp.float32) ** level_of(seeds[2], (NX, NY, NZ), ((0, 8), (1, 4)), -0.2, 0.2)), 0.25, 2.0)
    coarse_inverse = draw_coarse_inverse(jax.random.fold_in(seeds[4], 71), 0)
    return dict(source=source, reaction=reaction, conductance=conductance, coarse_inverse=coarse_inverse)


SHIFT = 0.06
KAPPA = 1.0

def sine_basis(extent):
    indices = jnp.arange(extent, dtype=jnp.float32) + 1.0
    angles = jnp.pi * indices[:, None] * indices[None, :] / (extent + 1)
    sine_table = jnp.sqrt(2.0 / (extent + 1)) * jnp.sin(angles)
    eigenvalues = 2.0 - 2.0 * jnp.cos(jnp.pi * indices / (extent + 1))
    return (sine_table, eigenvalues)

def harmonic(first, second):
    return 2.0 * first * second / (first + second)

def face_weights(padded_cond, conductance):
    face_x = harmonic(padded_cond[:-1, 1:-1], padded_cond[1:, 1:-1])
    face_y = harmonic(padded_cond[1:-1, :-1], padded_cond[1:-1, 1:])
    face_z = harmonic(conductance[:, :, :-1], conductance[:, :, 1:])
    return (face_x, face_y, face_z)

def operate(field, padded_field, reaction, face_x, face_y, face_z):
    result = reaction * field
    result = result + face_x[1:] * (field - padded_field[2:, 1:-1]) + face_x[:-1] * (field - padded_field[:-2, 1:-1])
    result = result + face_y[:, 1:] * (field - padded_field[1:-1, 2:]) + face_y[:, :-1] * (field - padded_field[1:-1, :-2])
    flux_z = face_z * (field[:, :, :-1] - field[:, :, 1:])
    return result + jnp.pad(flux_z, ((0, 0), (0, 0), (0, 1))) - jnp.pad(flux_z, ((0, 0), (0, 0), (1, 0)))

def transform_all(block, table_x, table_y, table_z):
    coeffs = jnp.einsum('rnyz,re->enyz', block, table_x, precision=lax.Precision.HIGHEST)
    coeffs = jnp.einsum('enyz,yb->enbz', coeffs, table_y, precision=lax.Precision.HIGHEST)
    return jnp.einsum('enbz,zc->enbc', coeffs, table_z, precision=lax.Precision.HIGHEST)

def local_solves(residual):
    extended = CX + 2 * W
    table_x, eigen_x = sine_basis(extended)
    table_y, eigen_y = sine_basis(CY)
    table_z, eigen_z = sine_basis(CZ)
    spectrum = SHIFT + KAPPA * (eigen_x[:, None, None, None] + eigen_y[None, None, :, None] + eigen_z[None, None, None, :])
    padded = jnp.pad(residual, ((W, W), (0, 0), (0, 0)))

    def one_slab(accumulated, position):
        offset_row = (position * CX).astype(jnp.int32)
        slab_block = lax.dynamic_slice_in_dim(padded, offset_row, extended, 0).reshape(extended, N_NARROW, CY, CZ)
        coeffs = transform_all(slab_block, table_x, table_y, table_z) / spectrum
        solved = transform_all(coeffs, table_x, table_y, table_z).reshape(extended, NY, NZ)
        current = lax.dynamic_slice_in_dim(accumulated, offset_row, extended, 0)
        return (lax.dynamic_update_slice_in_dim(accumulated, current + solved, offset_row, 0), None)
    accumulated, unused = lax.scan(one_slab, jnp.zeros_like(padded), jnp.arange(N_WIDE, dtype=jnp.int32))
    return accumulated[W:W + NX]

def coarse_part(residual, coarse_inverse):
    octant_means = residual.reshape(N_WIDE, 2, CX // 2, N_NARROW, 2, CY // 2, 2, CZ // 2).mean(axis=(2, 5, 7))
    ordered = octant_means.transpose(0, 2, 1, 3, 4).reshape(COARSE)
    correction = jnp.dot(coarse_inverse.reshape(COARSE, COARSE), ordered, precision=lax.Precision.HIGHEST)
    correction = correction.reshape(N_WIDE, N_NARROW, 2, 2, 2).transpose(0, 2, 1, 3, 4)
    spread = jnp.broadcast_to(correction[:, :, None, :, :, None, :, None], (N_WIDE, 2, CX // 2, N_NARROW, 2, CY // 2, 2, CZ // 2))
    return spread.reshape(NX, NY, NZ)

def reference(source, reaction, conductance, coarse_inverse):
    padded_cond = jnp.pad(conductance, ((1, 1), (1, 1), (0, 0)))
    face_x, face_y, face_z = face_weights(padded_cond, conductance)

    def apply_matrix(field):
        return operate(field, jnp.pad(field, ((1, 1), (1, 1), (0, 0))), reaction, face_x, face_y, face_z)

    def precondition(field):
        return local_solves(field) + coarse_part(field, coarse_inverse)
    solution = jnp.zeros_like(source)
    residual = source
    preconditioned = precondition(residual)
    direction = preconditioned
    gamma_now = jnp.sum(residual * preconditioned)
    for iteration in range(ITERS):
        image = apply_matrix(direction)
        step_size = gamma_now / jnp.sum(direction * image)
        solution = solution + step_size * direction
        residual = residual - step_size * image
        preconditioned = precondition(residual)
        gamma_next = jnp.sum(residual * preconditioned)
        direction = preconditioned + gamma_next / gamma_now * direction
        gamma_now = gamma_next
    return (solution, residual, direction)
```

```python
import functools

import jax
import jax.numpy as jnp
import numpy as np
from jax import lax
from jax.experimental import pallas as pl
from jax.experimental.pallas import tpu as pltpu
from jax.sharding import PartitionSpec as P

W = 8
PRIMAL = 8
SHIFT = 0.06
MESH = pl.DeviceIdType.MESH
f32 = jnp.float32
bf16 = jnp.bfloat16


def sine_basis(extent):
    indices = np.arange(extent, dtype=np.float64) + 1.0
    angles = np.pi * indices[:, None] * indices[None, :] / (extent + 1)
    table = np.sqrt(2.0 / (extent + 1)) * np.sin(angles)
    eigen = 2.0 - 2.0 * np.cos(np.pi * indices / (extent + 1))
    return table, eigen


def split(value):
    high = value.astype(bf16)
    return high, (value - high.astype(f32)).astype(bf16)


def harmonic(first, second):
    return 2.0 * first * second / (first + second)


def kernel(
    nw, nn, src, rea, con, cexp, tabz, taby, eigy, eigz, x_out, r_out, d_out,
    spec_r, spec_w0, spec_w1, own, total, tail, head, cp, inv, fx, fy, fylo, fz,
    z0, z1, w0, w1, chx, chy, cys, pqs, pqr, yr, hx, hy, hys, ga, gb, gc, gd,
    nsend, nrecv, gs1, gr1, gs2, gr2,
):
    bx, by, bz = src.shape
    iw, inn = lax.axis_index("wide"), lax.axis_index("narrow")
    place = {"wide": (iw, nw), "narrow": (inn, nn)}

    barrier = pltpu.get_barrier_semaphore()

    def greet(axis):
        me, count = place[axis]

        def one(k, carry):
            pl.semaphore_signal(
                barrier, inc=1, device_id={axis: lax.rem(me + k, count)}, device_id_type=MESH
            )
            return carry

        lax.fori_loop(1, count, one, 0)

    greet("wide")
    greet("narrow")
    pl.semaphore_wait(barrier, nw + nn - 2)

    class Shift:
        def __init__(self, source, target, slot, axis, step):
            me, count = place[axis]
            if step > 0:
                self.sends, self.gets = me < count - 1, me > 0
            else:
                self.sends, self.gets = me > 0, me < count - 1
            self.copy = pltpu.make_async_remote_copy(
                src_ref=source, dst_ref=target, send_sem=nsend.at[slot], recv_sem=nrecv.at[slot],
                device_id={axis: me + step}, device_id_type=MESH,
            )

        def start(self):
            @pl.when(self.sends)
            def _():
                self.copy.start()

        def arrive(self):
            @pl.when(self.gets)
            def _():
                self.copy.wait_recv()

        def leave(self):
            @pl.when(self.sends)
            def _():
                self.copy.wait_send()

    def pair(low_source, high_source, target, slot, axis):
        return (
            Shift(high_source, target.at[0], slot, axis, 1),
            Shift(low_source, target.at[1], slot + 1, axis, -1),
        )

    def each(copies, verb):
        for copy in copies:
            getattr(copy, verb)()

    class Gather:
        def __init__(self, ref, slot):
            self.ref, self.slot = ref, slot

        def near(self, k):
            return pltpu.make_async_remote_copy(
                src_ref=self.ref.at[iw, inn], dst_ref=self.ref.at[iw, inn],
                send_sem=gs1.at[self.slot, k], recv_sem=gr1.at[self.slot, k],
                device_id={"narrow": lax.rem(inn + k, nn)}, device_id_type=MESH,
            )

        def far(self, k):
            return pltpu.make_async_remote_copy(
                src_ref=self.ref.at[iw], dst_ref=self.ref.at[iw],
                send_sem=gs2.at[self.slot, k], recv_sem=gr2.at[self.slot, k],
                device_id={"wide": lax.rem(iw + k, nw)}, device_id_type=MESH,
            )

        def loop(self, count, step):
            def one(k, carry):
                step(k)
                return carry

            lax.fori_loop(1, count, one, 0)

        def first(self):
            self.loop(nn, lambda k: self.near(k).start())

        def second(self):
            self.loop(nn, lambda k: self.near(k).wait())
            self.loop(nw, lambda k: self.far(k).start())

        def finish(self):
            self.loop(nw, lambda k: self.far(k).wait())

    for edge, side in ((iw == 0, 0), (iw == nw - 1, 1)):
        @pl.when(edge)
        def _():
            blank = jnp.zeros((by, bz), f32)
            chx[side] = blank
            for turn in range(3):
                pqr[turn, side] = blank
                yr[turn, side] = blank
            for turn in range(2):
                hx[turn, side] = blank

    for edge, side in ((inn == 0, 0), (inn == nn - 1, 1)):
        @pl.when(edge)
        def _():
            blank = jnp.zeros((bx, bz), f32)
            chy[side] = blank
            for turn in range(2):
                hy[turn, side] = blank

    cys[0] = con[:, 0, :]
    cys[1] = con[:, by - 1, :]
    cond_x = pair(con.at[0], con.at[bx - 1], chx, 0, "wide")
    cond_y = pair(cys.at[0], cys.at[1], chy, 2, "narrow")
    each(cond_x + cond_y, "start")

    def fold8(value):
        return value.reshape(value.shape[0] // 8, 8, bz).sum(axis=0)

    half_y, half_x = by // 2, bx // 2
    zero8 = jnp.zeros((8, bz), f32)

    def post(ref, rows):
        for k, row in enumerate(rows):
            ref[iw, inn, pl.ds(k, 1), :] = jnp.sum(row, axis=0, keepdims=True)

    def means_of(field):
        rows = []
        for part in range(2):
            def one(x, carry):
                value = field[x]
                return carry[0] + fold8(value[:half_y]), carry[1] + fold8(value[half_y:])

            rows += list(lax.fori_loop(part * half_x, (part + 1) * half_x, one, (zero8, zero8)))
        return rows

    gather_a, gather_b, gather_c, gather_d = (
        Gather(ref, slot) for slot, ref in enumerate((ga, gb, gc, gd))
    )
    post(ga, means_of(src) + [zero8] * 4)
    gather_a.first()

    def along_z(value):
        high, low = split(value)
        both = jnp.dot(
            jnp.concatenate([high, low], axis=1), tabz[...], preferred_element_type=f32
        )
        return both[:, :bz] + both[:, bz:]

    def along_y(value):
        high, low = split(value)
        pairs = jnp.concatenate([high, low], axis=1)
        both = jnp.dot(
            taby[...], jnp.concatenate([pairs, pairs], axis=0), preferred_element_type=f32
        )
        return both[:, :bz] + both[:, bz:]

    step = 4

    def forward(field, out):
        def one(k, carry):
            rows = pl.ds(k * step, step)
            value = along_z(field[rows].reshape(step * by, bz))
            for j in range(step):
                out[k * step + j] = along_y(value[j * by : (j + 1) * by])
            return carry

        lax.fori_loop(0, bx // step, one, 0)

    chunk = by // 2
    on_left = (iw > 0).astype(f32)
    on_right = (iw < nw - 1).astype(f32)

    def chunks(work):
        def one(k, carry):
            work(pl.ds(pl.multiple_of(k * chunk, chunk), chunk))
            return carry

        lax.fori_loop(0, by // chunk, one, 0)

    def eliminate(rows):
        diagonal = 2.0 + SHIFT + eigy[rows, :] + eigz[...]
        last = 1.0 / diagonal
        cp[0, rows, :] = last
        for k in range(1, W + bx):
            last = 1.0 / (diagonal - last)
            cp[k, rows, :] = last
        inv[rows, :] = 1.0 / (1.0 - last * cp[W - 1, rows, :])

    chunks(eliminate)

    def solve(turn, prepare):
        def ends(rows):
            prepare(rows)
            value = jnp.zeros((chunk, bz), f32)
            for k in range(W):
                value = (spec_r[bx - W + k, rows, :] + value) * cp[k, rows, :]
                tail[k, rows, :] = value
            pqs[turn, 1, rows, :] = value
            value = jnp.zeros((chunk, bz), f32)
            for t in reversed(range(W)):
                value = (spec_r[t, rows, :] + value) * cp[W - 1 - t, rows, :]
                head[t, rows, :] = value
            pqs[turn, 0, rows, :] = value

        chunks(ends)
        rims = pair(pqs.at[turn, 0], pqs.at[turn, 1], pqr.at[turn], 4 + 4 * turn, "wide")
        each(rims, "start")
        yield
        each(rims, "arrive")

        def middle(rows):
            value = pqr[turn, 0, rows, :]
            for t in range(bx):
                value = (spec_r[t, rows, :] + value) * cp[W + t, rows, :]
                if t < bx - 1:
                    own[t, rows, :] = value
            value = (value + cp[W + bx - 1, rows, :] * pqr[turn, 1, rows, :]) * inv[rows, :]
            own[bx - 1, rows, :] = value
            for t in reversed(range(bx - 1)):
                value = own[t, rows, :] + cp[W + t, rows, :] * value
                own[t, rows, :] = value

        chunks(middle)
        backs = pair(own.at[0], own.at[bx - 1], yr.at[turn], 6 + 4 * turn, "wide")
        each(backs, "start")
        yield
        each(backs, "arrive")

        def fold(rows):
            value = yr[turn, 1, rows, :]
            for k in reversed(range(W)):
                value = tail[k, rows, :] + cp[k, rows, :] * value
                t = bx - W + k
                total[t, rows, :] = own[t, rows, :] + on_right * value
            value = yr[turn, 0, rows, :]
            for t in range(W):
                value = head[t, rows, :] + cp[W - 1 - t, rows, :] * value
                total[t, rows, :] = own[t, rows, :] + on_left * value

        chunks(fold)
        each(rims, "leave")
        each(backs, "leave")
        yield

    lanes = lax.broadcasted_iota(jnp.int32, (1, bz), 1)

    def inverse(correction, out):
        for part in range(2):
            spread = []
            for side in range(2):
                o = part * 4 + side * 2
                row = jnp.where(lanes < bz // 2, correction[o], correction[o + 1])
                spread.append(jnp.broadcast_to(row, (half_y, bz)))
            spread = jnp.concatenate(spread, axis=0)

            def one(k, carry):
                value = jnp.concatenate(
                    [along_y(total[k * step + j]) for j in range(step)], axis=0
                )
                value = along_z(value)
                for j in range(step):
                    out[k * step + j] = value[j * by : (j + 1) * by] + spread
                return carry

            lax.fori_loop(part * (half_x // step), (part + 1) * (half_x // step), one, 0)

    scale = 1.0 / (half_x * half_y * (bz // 2))

    def everything(value):
        return jnp.sum(jnp.sum(value, axis=0, keepdims=True), axis=1, keepdims=True)

    def correct(ref):
        message = ref[...].reshape(nw * nn, 8, bz)
        return [everything(jnp.sum(message * cexp[o], axis=0)) * scale for o in range(PRIMAL)]

    def dots(ref):
        whole = jnp.sum(ref[...].reshape(nw * nn, 8, bz), axis=0)
        return [jnp.sum(whole[k : k + 1], axis=1, keepdims=True) for k in range(4, 7)]

    index_y = lax.broadcasted_iota(jnp.int32, (by, bz), 0)

    def shifted_down(value, low):
        return jnp.where(index_y == 0, low, pltpu.roll(value, 1, 0))

    def shifted_up(value, high):
        return jnp.where(index_y == by - 1, high, pltpu.roll(value, by - 1, 0))

    def weights():
        each(cond_x + cond_y, "arrive")
        index_z = lax.broadcasted_iota(jnp.int32, (by, bz), 1)
        fx[0] = harmonic(chx[0], con[0])
        fx[bx] = harmonic(con[bx - 1], chx[1])

        def one(x, carry):
            value = con[x]
            fy[x] = harmonic(value, shifted_up(value, chy[1, pl.ds(x, 1), :]))
            fz[x] = jnp.where(
                index_z == bz - 1, 0.0, harmonic(value, pltpu.roll(value, bz - 1, 1))
            )
            return carry

        def between(x, carry):
            fx[x] = harmonic(con[x - 1], con[x])
            return carry

        lax.fori_loop(0, bx, one, 0)
        lax.fori_loop(1, bx, between, 0)
        fylo[...] = harmonic(cys[0], chy[0])
        each(cond_x + cond_y, "leave")

    def apply(turn, field, out, inner):
        hys[turn, 0] = field[:, 0, :]
        hys[turn, 1] = field[:, by - 1, :]
        slot = 16 + 4 * turn
        layers = pair(field.at[0], field.at[bx - 1], hx.at[turn], slot, "wide") + pair(
            hys.at[turn, 0], hys.at[turn, 1], hy.at[turn], slot + 2, "narrow"
        )
        each(layers, "start")
        if turn == 0:
            weights()
        each(layers, "arrive")

        def point(x, below, above):
            value = field[x]
            result = rea[x] * value
            result = result + fx[x + 1] * (value - above) + fx[x] * (value - below)
            flux = fy[x] * (value - shifted_up(value, hy[turn, 1, pl.ds(x, 1), :]))
            low = fylo[pl.ds(x, 1), :] * (hy[turn, 0, pl.ds(x, 1), :] - value[0:1])
            result = result + flux - shifted_down(flux, low)
            flux = fz[x] * (value - pltpu.roll(value, bz - 1, 1))
            result = result + flux - pltpu.roll(flux, 1, 1)
            out[x] = result
            return value, result

        sums, products = [], [zero8] * 3

        def gather_up(x, below, above, carry):
            value, result = point(x, below, above)
            extra = inner(x, value, result)
            return (
                carry[0] + fold8(result[:half_y]), carry[1] + fold8(result[half_y:]),
            ) + tuple(c + fold8(e) for c, e in zip(carry[2:], extra))

        for part in range(2):
            carry = (zero8, zero8) + tuple(products)
            if part == 0:
                carry = gather_up(0, hx[turn, 0], field[1], carry)
                low, high = 1, half_x
            else:
                low, high = half_x, bx - 1
            carry = lax.fori_loop(
                low, high, lambda x, c: gather_up(x, field[x - 1], field[x + 1], c), carry
            )
            if part == 1:
                carry = gather_up(bx - 1, field[bx - 2], hx[turn, 1], carry)
            sums += [carry[0], carry[1]]
            products = list(carry[2:])
        each(layers, "leave")
        return sums + products + [zero8]

    def local(turn, prepare, between=None):
        stages = solve(turn, prepare)
        next(stages)
        if between is not None:
            between()
        next(stages)
        next(stages)

    forward(src, spec_r)
    gather_a.second()
    local(0, lambda rows: None)
    gather_a.finish()
    coarse = correct(ga)
    inverse(coarse, z0)
    post(gb, apply(0, z0, w0, lambda x, v, a: (src[x] * v, v * a, zero8)))
    gather_b.first()

    forward(w0, spec_w0)
    gather_b.second()
    gather_b.finish()
    gamma0, delta0, _ = dots(gb)
    alpha0 = gamma0 / delta0

    def first_step(rows):
        for t in range(bx):
            spec_r[t, rows, :] = spec_r[t, rows, :] - alpha0 * spec_w0[t, rows, :]

    local(1, first_step)
    coarse_b = correct(gb)
    coarse = [a - alpha0 * b for a, b in zip(coarse, coarse_b)]
    inverse(coarse, z1)

    def inner(x, value, result):
        image = w0[x]
        return (src[x] - alpha0 * image) * value, value * result, value * image

    post(gc, apply(1, z1, w1, inner))
    gather_c.first()

    forward(w1, spec_w1)
    gather_c.second()
    gather_c.finish()
    gamma1, own1, cross1 = dots(gc)
    beta1 = gamma1 / gamma0
    alpha1 = gamma1 / (own1 + 2.0 * beta1 * cross1 + beta1 * beta1 * delta0)

    def second_step(rows):
        for t in range(bx):
            image = spec_w1[t, rows, :] + beta1 * spec_w0[t, rows, :]
            spec_r[t, rows, :] = spec_r[t, rows, :] - alpha1 * image

    def results():
        def one(x, carry):
            direction = z1[x] + beta1 * z0[x]
            x_out[x] = alpha0 * z0[x] + alpha1 * direction
            image = w0[x]
            r_out[x] = (src[x] - alpha0 * image) - alpha1 * (w1[x] + beta1 * image)
            z1[x] = direction
            return carry

        lax.fori_loop(0, bx, one, 0)

    local(2, second_step, results)
    coarse_c = correct(gc)
    coarse = [a - alpha1 * (c + beta1 * b) for a, b, c in zip(coarse, coarse_b, coarse_c)]
    inverse(coarse, w1)
    product = lax.fori_loop(0, bx, lambda x, c: c + fold8(r_out[x] * w1[x]), zero8)
    post(gd, [zero8] * 4 + [product] + [zero8] * 3)
    gather_d.first()
    gather_d.second()
    gather_d.finish()
    beta2 = dots(gd)[0] / gamma1

    def last(x, carry):
        d_out[x] = w1[x] + beta2 * z1[x]
        return carry

    lax.fori_loop(0, bx, last, 0)


def body(nw, nn, source, reaction, conductance, coarse_inverse):
    bx, by, bz = source.shape
    table_y, eigen_y = sine_basis(by)
    table_z, eigen_z = sine_basis(bz)

    def parts(table):
        table = np.asarray(table, np.float32)
        high = table.astype(jnp.bfloat16)
        low = (table - high.astype(np.float32)).astype(jnp.bfloat16)
        return np.concatenate([high, low], axis=1)

    tab_y = parts(table_y)
    tab_z = parts(table_z)
    tab_z = np.concatenate([tab_z, tab_z], axis=0)
    rows = coarse_inverse.reshape(PRIMAL, nw * nn, 4, 2, 1)
    rows = jnp.broadcast_to(rows, (PRIMAL, nw * nn, 4, 2, bz // 2)).reshape(
        PRIMAL, nw * nn, 4, bz
    )
    rows = jnp.pad(rows, ((0, 0), (0, 0), (0, 4), (0, 0)))
    block = (bx, by, bz)
    layer = (by, bz)

    def vm(*shape):
        return pltpu.VMEM(shape, f32)

    scratch = [
        vm(*block), vm(*block), vm(*block), vm(*block), vm(*block),
        vm(W, *layer), vm(W, *layer), vm(W + bx, *layer), vm(*layer),
        vm(bx + 1, *layer), vm(*block), vm(bx, bz), vm(*block),
        vm(*block), vm(*block), vm(*block), vm(*block),
        vm(2, *layer), vm(2, bx, bz), vm(2, bx, bz),
        vm(3, 2, *layer), vm(3, 2, *layer), vm(3, 2, *layer),
        vm(2, 2, *layer), vm(2, 2, bx, bz), vm(2, 2, bx, bz),
        vm(nw, nn, 8, bz), vm(nw, nn, 8, bz), vm(nw, nn, 8, bz), vm(nw, nn, 8, bz),
        pltpu.SemaphoreType.DMA((24,)), pltpu.SemaphoreType.DMA((24,)),
        pltpu.SemaphoreType.DMA((4, nn)), pltpu.SemaphoreType.DMA((4, nn)),
        pltpu.SemaphoreType.DMA((4, nw)), pltpu.SemaphoreType.DMA((4, nw)),
    ]
    spec = pl.BlockSpec(memory_space=pltpu.VMEM)
    return pl.pallas_call(
        functools.partial(kernel, nw, nn),
        out_shape=[jax.ShapeDtypeStruct(block, f32)] * 3,
        in_specs=[spec] * 8,
        out_specs=[spec] * 3,
        scratch_shapes=scratch,
        compiler_params=pltpu.CompilerParams(
            collective_id=0, has_side_effects=True, vmem_limit_bytes=52 * 1024 * 1024
        ),
    )(
        source, reaction, conductance, rows,
        jnp.asarray(tab_z), jnp.asarray(tab_y),
        jnp.asarray(eigen_y.reshape(-1, 1), f32), jnp.asarray(eigen_z.reshape(1, -1), f32),
    )


def solution(mesh):
    grid = P("wide", "narrow", None)
    return jax.shard_map(
        functools.partial(body, mesh.shape["wide"], mesh.shape["narrow"]),
        mesh=mesh,
        in_specs=(grid, grid, grid, P("wide", "narrow", None, None)),
        out_specs=(grid, grid, grid),
        check_vma=False,
    )
```

```python
import functools

import jax
import jax.numpy as jnp
import numpy as np
from jax import lax
from jax.experimental import pallas as pl
from jax.experimental.pallas import tpu as pltpu
from jax.sharding import PartitionSpec as P

W = 8
PRIMAL = 8
SHIFT = 0.06
MESH = pl.DeviceIdType.MESH
f32 = jnp.float32
bf16 = jnp.bfloat16


def sine_basis(extent):
    indices = np.arange(extent, dtype=np.float64) + 1.0
    angles = np.pi * indices[:, None] * indices[None, :] / (extent + 1)
    table = np.sqrt(2.0 / (extent + 1)) * np.sin(angles)
    eigen = 2.0 - 2.0 * np.cos(np.pi * indices / (extent + 1))
    return table, eigen


def split(value):
    high = value.astype(bf16)
    return high, (value - high.astype(f32)).astype(bf16)


def harmonic(first, second):
    return 2.0 * first * second / (first + second)


def kernel(
    nw, nn, src, rea, con, cinv, tabz, taby, eigy, eigz, x_out, r_out, d_out,
    spec, own, total, total0, total1, tail, head, cp, inv, fx, fy, fylo, fz,
    z0, z1, w0, w1, chx, chy, cys, pqs, pqr, yr, hx, hy, hys, ga, gb, gc, gd,
    wide_rows, nsend, nrecv, gs1, gr1, gs2, gr2,
):
    bx, by, bz = src.shape
    iw, inn = lax.axis_index("wide"), lax.axis_index("narrow")
    place = {"wide": (iw, nw), "narrow": (inn, nn)}

    barrier = pltpu.get_barrier_semaphore()

    def greet(axis):
        me, count = place[axis]

        def one(k, carry):
            pl.semaphore_signal(
                barrier, inc=1, device_id={axis: lax.rem(me + k, count)}, device_id_type=MESH
            )
            return carry

        lax.fori_loop(1, count, one, 0)

    greet("wide")
    greet("narrow")
    pl.semaphore_wait(barrier, nw + nn - 2)

    class Shift:
        def __init__(self, source, target, slot, axis, step):
            me, count = place[axis]
            if step > 0:
                self.sends, self.gets = me < count - 1, me > 0
            else:
                self.sends, self.gets = me > 0, me < count - 1
            self.copy = pltpu.make_async_remote_copy(
                src_ref=source, dst_ref=target, send_sem=nsend.at[slot], recv_sem=nrecv.at[slot],
                device_id={axis: me + step}, device_id_type=MESH,
            )

        def start(self):
            @pl.when(self.sends)
            def _():
                self.copy.start()

        def arrive(self):
            @pl.when(self.gets)
            def _():
                self.copy.wait_recv()

        def leave(self):
            @pl.when(self.sends)
            def _():
                self.copy.wait_send()

    def pair(low_source, high_source, target, slot, axis):
        return (
            Shift(high_source, target.at[0], slot, axis, 1),
            Shift(low_source, target.at[1], slot + 1, axis, -1),
        )

    def each(copies, verb):
        for copy in copies:
            getattr(copy, verb)()

    class Gather:
        def __init__(self, ref, slot):
            self.ref, self.slot = ref, slot

        def near(self, k):
            return pltpu.make_async_remote_copy(
                src_ref=self.ref.at[iw, inn], dst_ref=self.ref.at[iw, inn],
                send_sem=gs1.at[self.slot, k], recv_sem=gr1.at[self.slot, k],
                device_id={"narrow": lax.rem(inn + k, nn)}, device_id_type=MESH,
            )

        def far(self, k):
            return pltpu.make_async_remote_copy(
                src_ref=self.ref.at[iw], dst_ref=self.ref.at[iw],
                send_sem=gs2.at[self.slot, k], recv_sem=gr2.at[self.slot, k],
                device_id={"wide": lax.rem(iw + k, nw)}, device_id_type=MESH,
            )

        def loop(self, count, step):
            def one(k, carry):
                step(k)
                return carry

            lax.fori_loop(1, count, one, 0)

        def first(self):
            self.loop(nn, lambda k: self.near(k).start())

        def second(self):
            self.loop(nn, lambda k: self.near(k).wait())
            self.loop(nw, lambda k: self.far(k).start())

        def finish(self):
            self.loop(nw, lambda k: self.far(k).wait())

    for edge, side in ((iw == 0, 0), (iw == nw - 1, 1)):
        @pl.when(edge)
        def _():
            blank = jnp.zeros((by, bz), f32)
            chx[side] = blank
            for turn in range(3):
                pqr[turn, side] = blank
                yr[turn, side] = blank
            for turn in range(2):
                hx[turn, side] = blank

    for edge, side in ((inn == 0, 0), (inn == nn - 1, 1)):
        @pl.when(edge)
        def _():
            blank = jnp.zeros((bx, bz), f32)
            chy[side] = blank
            for turn in range(2):
                hy[turn, side] = blank

    cys[0] = con[:, 0, :]
    cys[1] = con[:, by - 1, :]
    cond_x = pair(con.at[0], con.at[bx - 1], chx, 0, "wide")
    cond_y = pair(cys.at[0], cys.at[1], chy, 2, "narrow")
    each(cond_x + cond_y, "start")

    def fold8(value):
        return value.reshape(value.shape[0] // 8, 8, bz).sum(axis=0)

    half_y, half_x = by // 2, bx // 2
    zero8 = jnp.zeros((8, bz), f32)

    def post(ref, rows):
        for k, row in enumerate(rows):
            ref[iw, inn, pl.ds(k, 1), :] = jnp.sum(row, axis=0, keepdims=True)

    def means_of(field):
        rows = []
        for part in range(2):
            def one(x, carry):
                value = field[x]
                return carry[0] + fold8(value[:half_y]), carry[1] + fold8(value[half_y:])

            rows += list(lax.fori_loop(part * half_x, (part + 1) * half_x, one, (zero8, zero8)))
        return rows

    gather_a, gather_b, gather_c, gather_d = (
        Gather(ref, slot) for slot, ref in enumerate((ga, gb, gc, gd))
    )
    post(ga, means_of(src) + [zero8] * 4)
    gather_a.first()

    def along_z(value):
        high, low = split(value)
        both = jnp.dot(
            jnp.concatenate([high, low], axis=1), tabz[...], preferred_element_type=f32
        )
        return both[:, :bz] + both[:, bz:]

    def along_y(value):
        high, low = split(value)
        pairs = jnp.concatenate([high, low], axis=1)
        both = jnp.dot(
            taby[...], jnp.concatenate([pairs, pairs], axis=0), preferred_element_type=f32
        )
        return both[:, :bz] + both[:, bz:]

    step = bx

    def forward(field, out):
        def one(k, carry):
            rows = pl.ds(k * step, step)
            value = along_z(field[rows].reshape(step * by, bz))
            for j in range(step):
                out[k * step + j] = along_y(value[j * by : (j + 1) * by])
            return carry

        lax.fori_loop(0, bx // step, one, 0)

    chunk = by // 2
    on_left = (iw > 0).astype(f32)
    on_right = (iw < nw - 1).astype(f32)

    def chunks(work):
        def one(k, carry):
            work(pl.ds(pl.multiple_of(k * chunk, chunk), chunk))
            return carry

        lax.fori_loop(0, by // chunk, one, 0)

    def eliminate(rows):
        diagonal = 2.0 + SHIFT + eigy[rows, :] + eigz[...]
        last = 1.0 / diagonal
        cp[0, rows, :] = last
        for k in range(1, W + bx):
            last = 1.0 / (diagonal - last)
            cp[k, rows, :] = last
        inv[rows, :] = 1.0 / (1.0 - last * cp[W - 1, rows, :])

    chunks(eliminate)

    def solve(turn, out):
        def ends(rows):
            value = jnp.zeros((chunk, bz), f32)
            for k in range(W):
                value = (spec[bx - W + k, rows, :] + value) * cp[k, rows, :]
                tail[k, rows, :] = value
            pqs[turn, 1, rows, :] = value
            value = jnp.zeros((chunk, bz), f32)
            for t in reversed(range(W)):
                value = (spec[t, rows, :] + value) * cp[W - 1 - t, rows, :]
                head[t, rows, :] = value
            pqs[turn, 0, rows, :] = value

        chunks(ends)
        rims = pair(pqs.at[turn, 0], pqs.at[turn, 1], pqr.at[turn], 4 + 4 * turn, "wide")
        each(rims, "start")
        yield
        each(rims, "arrive")

        def middle(rows):
            value = pqr[turn, 0, rows, :]
            for t in range(bx):
                value = (spec[t, rows, :] + value) * cp[W + t, rows, :]
                if t < bx - 1:
                    own[t, rows, :] = value
            value = (value + cp[W + bx - 1, rows, :] * pqr[turn, 1, rows, :]) * inv[rows, :]
            own[bx - 1, rows, :] = value
            for t in reversed(range(bx - 1)):
                value = own[t, rows, :] + cp[W + t, rows, :] * value
                own[t, rows, :] = value

        chunks(middle)
        backs = pair(own.at[0], own.at[bx - 1], yr.at[turn], 6 + 4 * turn, "wide")
        each(backs, "start")
        yield
        each(backs, "arrive")

        def fold(rows):
            value = yr[turn, 1, rows, :]
            for k in reversed(range(W)):
                value = tail[k, rows, :] + cp[k, rows, :] * value
                t = bx - W + k
                out[t, rows, :] = own[t, rows, :] + on_right * value
            value = yr[turn, 0, rows, :]
            for t in range(W):
                value = head[t, rows, :] + cp[W - 1 - t, rows, :] * value
                out[t, rows, :] = own[t, rows, :] + on_left * value

        chunks(fold)
        each(rims, "leave")
        each(backs, "leave")
        yield

    lanes = lax.broadcasted_iota(jnp.int32, (1, bz), 1)

    def inverse(correction, out, combine):
        spread = []
        for o in range(0, PRIMAL, 2):
            row = jnp.where(lanes < bz // 2, correction[o], correction[o + 1])
            spread.append(jnp.broadcast_to(row, (half_y, bz)))
        spread = [jnp.concatenate(spread[o : o + 2], axis=0) for o in (0, 2)]
        value = along_z(jnp.concatenate([along_y(combine(x)) for x in range(bx)], axis=0))
        for x in range(bx):
            out[x] = value[x * by : (x + 1) * by] + spread[x // half_x]

    scale = 1.0 / (half_x * half_y * (bz // 2))

    def correct(ref):
        both = jnp.dot(
            wide_rows[...], ref[...].reshape(nw * nn * 8, bz),
            precision=lax.Precision.HIGHEST, preferred_element_type=f32,
        )
        upper = lax.broadcasted_iota(jnp.int32, (2 * PRIMAL, bz), 1) >= bz // 2
        second = lax.broadcasted_iota(jnp.int32, (2 * PRIMAL, bz), 0) >= PRIMAL
        both = jnp.sum(jnp.where(upper == second, both, 0.0), axis=1, keepdims=True)
        both = (both[:PRIMAL] + both[PRIMAL:]) * scale
        return [both[o : o + 1] for o in range(PRIMAL)]

    def lay_out():
        block = 128
        entry = lax.broadcasted_iota(jnp.int32, (block, block), 0)
        place_of = lax.broadcasted_iota(jnp.int32, (block, block), 1)
        device, row = place_of // 8, place_of % 8
        for side in range(2):
            chosen = jnp.where((row < 4) & (entry == device * 8 + 2 * row + side), 1.0, 0.0)
            for k in range(nw * nn * 8 // block):
                columns = slice(k * block, (k + 1) * block)
                wide_rows[side * PRIMAL : (side + 1) * PRIMAL, columns] = jnp.dot(
                    cinv[0, 0, :, columns], chosen.astype(f32),
                    precision=lax.Precision.HIGHEST, preferred_element_type=f32,
                )

    lay_out()

    def dots(ref):
        whole = jnp.sum(ref[...].reshape(nw * nn, 8, bz), axis=0)
        return [jnp.sum(whole[k : k + 1], axis=1, keepdims=True) for k in range(4, 7)]

    index_y = lax.broadcasted_iota(jnp.int32, (by, bz), 0)

    def shifted_down(value, low):
        return jnp.where(index_y == 0, low, pltpu.roll(value, 1, 0))

    def shifted_up(value, high):
        return jnp.where(index_y == by - 1, high, pltpu.roll(value, by - 1, 0))

    def weights():
        each(cond_x + cond_y, "arrive")
        index_z = lax.broadcasted_iota(jnp.int32, (by, bz), 1)
        fx[0] = harmonic(chx[0], con[0])
        fx[bx] = harmonic(con[bx - 1], chx[1])

        def one(x, carry):
            value = con[x]
            fy[x] = harmonic(value, shifted_up(value, chy[1, pl.ds(x, 1), :]))
            fz[x] = jnp.where(
                index_z == bz - 1, 0.0, harmonic(value, pltpu.roll(value, bz - 1, 1))
            )
            return carry

        def between(x, carry):
            fx[x] = harmonic(con[x - 1], con[x])
            return carry

        lax.fori_loop(0, bx, one, 0)
        lax.fori_loop(1, bx, between, 0)
        fylo[...] = harmonic(cys[0], chy[0])
        each(cond_x + cond_y, "leave")

    def apply(turn, field, out, inner):
        hys[turn, 0] = field[:, 0, :]
        hys[turn, 1] = field[:, by - 1, :]
        slot = 16 + 4 * turn
        layers = pair(field.at[0], field.at[bx - 1], hx.at[turn], slot, "wide") + pair(
            hys.at[turn, 0], hys.at[turn, 1], hy.at[turn], slot + 2, "narrow"
        )
        each(layers, "start")
        each(layers, "arrive")

        def point(x, below, above):
            value = field[x]
            result = rea[x] * value
            result = result + fx[x + 1] * (value - above) + fx[x] * (value - below)
            flux = fy[x] * (value - shifted_up(value, hy[turn, 1, pl.ds(x, 1), :]))
            low = fylo[pl.ds(x, 1), :] * (hy[turn, 0, pl.ds(x, 1), :] - value[0:1])
            result = result + flux - shifted_down(flux, low)
            flux = fz[x] * (value - pltpu.roll(value, bz - 1, 1))
            result = result + flux - pltpu.roll(flux, 1, 1)
            out[x] = result
            return value, result

        sums, products = [], [zero8] * 3

        def gather_up(x, below, above, carry):
            value, result = point(x, below, above)
            extra = inner(x, value, result)
            return (
                carry[0] + fold8(result[:half_y]), carry[1] + fold8(result[half_y:]),
            ) + tuple(c + fold8(e) for c, e in zip(carry[2:], extra))

        for part in range(2):
            carry = (zero8, zero8) + tuple(products)
            if part == 0:
                carry = gather_up(0, hx[turn, 0], field[1], carry)
                low, high = 1, half_x
            else:
                low, high = half_x, bx - 1
            carry = lax.fori_loop(
                low, high, lambda x, c: gather_up(x, field[x - 1], field[x + 1], c), carry,
                    unroll=True,
            )
            if part == 1:
                carry = gather_up(bx - 1, field[bx - 2], hx[turn, 1], carry)
            sums += [carry[0], carry[1]]
            products = list(carry[2:])
        each(layers, "leave")
        return sums + products + [zero8]

    def local(turn, out, gather, between):
        stages = solve(turn, out)
        next(stages)
        gather.second()
        next(stages)
        between()
        next(stages)
        gather.finish()

    forward(src, spec)
    local(0, total, gather_a, weights)
    coarse = correct(ga)
    inverse(coarse, z0, lambda x: total[x])
    post(gb, apply(0, z0, w0, lambda x, v, a: (src[x] * v, v * a, zero8)))
    gather_b.first()

    forward(w0, spec)
    local(1, total0, gather_b, lambda: None)
    gamma0, delta0, _ = dots(gb)
    alpha0 = gamma0 / delta0
    coarse_b = correct(gb)
    coarse = [a - alpha0 * b for a, b in zip(coarse, coarse_b)]

    def first_step(x):
        value = total[x] - alpha0 * total0[x]
        total[x] = value
        return value

    inverse(coarse, z1, first_step)

    def inner(x, value, result):
        image = w0[x]
        return (src[x] - alpha0 * image) * value, value * result, value * image

    post(gc, apply(1, z1, w1, inner))
    gather_c.first()

    forward(w1, spec)
    local(2, total1, gather_c, lambda: None)
    gamma1, own1, cross1 = dots(gc)
    beta1 = gamma1 / gamma0
    alpha1 = gamma1 / (own1 + 2.0 * beta1 * cross1 + beta1 * beta1 * delta0)

    def results():
        def one(x, carry):
            direction = z1[x] + beta1 * z0[x]
            x_out[x] = alpha0 * z0[x] + alpha1 * direction
            image = w0[x]
            r_out[x] = (src[x] - alpha0 * image) - alpha1 * (w1[x] + beta1 * image)
            z1[x] = direction
            return carry

        lax.fori_loop(0, bx, one, 0, unroll=4)

    coarse_c = correct(gc)
    coarse = [a - alpha1 * (c + beta1 * b) for a, b, c in zip(coarse, coarse_b, coarse_c)]
    inverse(
        coarse, d_out,
        lambda x: total[x] - alpha1 * (total1[x] + beta1 * total0[x]),
    )

    def last_product(x, carry):
        image = w0[x]
        remaining = (src[x] - alpha0 * image) - alpha1 * (w1[x] + beta1 * image)
        return carry + fold8(remaining * d_out[x])

    product = lax.fori_loop(0, bx, last_product, zero8, unroll=4)
    post(gd, [zero8] * 4 + [product] + [zero8] * 3)
    gather_d.first()
    gather_d.second()
    results()
    gather_d.finish()
    beta2 = dots(gd)[0] / gamma1

    def last(x, carry):
        d_out[x] = d_out[x] + beta2 * z1[x]
        return carry

    lax.fori_loop(0, bx, last, 0, unroll=4)


def body(nw, nn, source, reaction, conductance, coarse_inverse):
    bx, by, bz = source.shape
    table_y, eigen_y = sine_basis(by)
    table_z, eigen_z = sine_basis(bz)

    def parts(table):
        table = np.asarray(table, np.float32)
        high = table.astype(jnp.bfloat16)
        low = (table - high.astype(np.float32)).astype(jnp.bfloat16)
        return np.concatenate([high, low], axis=1)

    tab_y = parts(table_y)
    tab_z = parts(table_z)
    tab_z = np.concatenate([tab_z, tab_z], axis=0)
    block = (bx, by, bz)
    layer = (by, bz)

    def vm(*shape):
        return pltpu.VMEM(shape, f32)

    scratch = [
        vm(*block), vm(*block), vm(*block), vm(*block), vm(*block),
        vm(W, *layer), vm(W, *layer), vm(W + bx, *layer), vm(*layer),
        vm(bx + 1, *layer), vm(*block), vm(bx, bz), vm(*block),
        vm(*block), vm(*block), vm(*block), vm(*block),
        vm(2, *layer), vm(2, bx, bz), vm(2, bx, bz),
        vm(3, 2, *layer), vm(3, 2, *layer), vm(3, 2, *layer),
        vm(2, 2, *layer), vm(2, 2, bx, bz), vm(2, 2, bx, bz),
        vm(nw, nn, 8, bz), vm(nw, nn, 8, bz), vm(nw, nn, 8, bz), vm(nw, nn, 8, bz),
        vm(2 * PRIMAL, nw * nn * 8),
        pltpu.SemaphoreType.DMA((24,)), pltpu.SemaphoreType.DMA((24,)),
        pltpu.SemaphoreType.DMA((4, nn)), pltpu.SemaphoreType.DMA((4, nn)),
        pltpu.SemaphoreType.DMA((4, nw)), pltpu.SemaphoreType.DMA((4, nw)),
    ]
    spec = pl.BlockSpec(memory_space=pltpu.VMEM)
    return pl.pallas_call(
        functools.partial(kernel, nw, nn),
        out_shape=[jax.ShapeDtypeStruct(block, f32)] * 3,
        in_specs=[spec] * 8,
        out_specs=[spec] * 3,
        scratch_shapes=scratch,
        compiler_params=pltpu.CompilerParams(
            collective_id=0, has_side_effects=True, vmem_limit_bytes=32 * 1024 * 1024
        ),
    )(
        source, reaction, conductance, coarse_inverse,
        jnp.asarray(tab_z), jnp.asarray(tab_y),
        jnp.asarray(eigen_y.reshape(-1, 1), f32), jnp.asarray(eigen_z.reshape(1, -1), f32),
    )


def solution(mesh):
    grid = P("wide", "narrow", None)
    return jax.shard_map(
        functools.partial(body, mesh.shape["wide"], mesh.shape["narrow"]),
        mesh=mesh,
        in_specs=(grid, grid, grid, P("wide", "narrow", None, None)),
        out_specs=(grid, grid, grid),
        check_vma=False,
    )
```

```python
import functools

import jax
import jax.numpy as jnp
import numpy as np
from jax import lax
from jax.experimental import pallas as pl
from jax.experimental.pallas import tpu as pltpu
from jax.sharding import PartitionSpec as P

W = 8
PRIMAL = 8
SHIFT = 0.06
MESH = pl.DeviceIdType.MESH
f32 = jnp.float32
bf16 = jnp.bfloat16


def sine_basis(extent):
    indices = np.arange(extent, dtype=np.float64) + 1.0
    angles = np.pi * indices[:, None] * indices[None, :] / (extent + 1)
    table = np.sqrt(2.0 / (extent + 1)) * np.sin(angles)
    eigen = 2.0 - 2.0 * np.cos(np.pi * indices / (extent + 1))
    return table, eigen


def split(value):
    high = value.astype(bf16)
    return high, (value - high.astype(f32)).astype(bf16)


def harmonic(first, second):
    return 2.0 * first * second / (first + second)


def kernel(
    nw, nn, src, rea, con, cinv, tabz, taby, eigy, eigz, x_out, r_out, d_out,
    spec, spec0, spec1, own, total, total0, total1, tail, head, cp, inv, fx, fy, fylo, fyhi, fz,
    z0, z1, w0, w1, chx, chy, cys, pqs, pqr, yr, hx, hy, hys, ga, gb, gc, gd,
    wide_rows, nsend, nrecv, gs1, gr1, gs2, gr2,
):
    bx, by, bz = src.shape
    iw, inn = lax.axis_index("wide"), lax.axis_index("narrow")
    place = {"wide": (iw, nw), "narrow": (inn, nn)}

    barrier = pltpu.get_barrier_semaphore()

    def greet(axis):
        me, count = place[axis]

        def one(k, carry):
            pl.semaphore_signal(
                barrier, inc=1, device_id={axis: lax.rem(me + k, count)}, device_id_type=MESH
            )
            return carry

        lax.fori_loop(1, count, one, 0)

    greet("wide")
    greet("narrow")

    class Shift:
        def __init__(self, source, target, slot, axis, step):
            me, count = place[axis]
            if step > 0:
                self.sends, self.gets = me < count - 1, me > 0
            else:
                self.sends, self.gets = me > 0, me < count - 1
            self.copy = pltpu.make_async_remote_copy(
                src_ref=source, dst_ref=target, send_sem=nsend.at[slot], recv_sem=nrecv.at[slot],
                device_id={axis: me + step}, device_id_type=MESH,
            )

        def start(self):
            @pl.when(self.sends)
            def _():
                self.copy.start()

        def arrive(self):
            @pl.when(self.gets)
            def _():
                self.copy.wait_recv()

        def leave(self):
            @pl.when(self.sends)
            def _():
                self.copy.wait_send()

    def pair(low_source, high_source, target, slot, axis):
        return (
            Shift(high_source, target.at[0], slot, axis, 1),
            Shift(low_source, target.at[1], slot + 1, axis, -1),
        )

    def each(copies, verb):
        for copy in copies:
            getattr(copy, verb)()

    class Gather:
        def __init__(self, ref, slot):
            self.ref, self.slot = ref, slot

        def near(self, k):
            return pltpu.make_async_remote_copy(
                src_ref=self.ref.at[iw, inn], dst_ref=self.ref.at[iw, inn],
                send_sem=gs1.at[self.slot, k], recv_sem=gr1.at[self.slot, k],
                device_id={"narrow": lax.rem(inn + k, nn)}, device_id_type=MESH,
            )

        def far(self, k):
            return pltpu.make_async_remote_copy(
                src_ref=self.ref.at[iw], dst_ref=self.ref.at[iw],
                send_sem=gs2.at[self.slot, k], recv_sem=gr2.at[self.slot, k],
                device_id={"wide": lax.rem(iw + k, nw)}, device_id_type=MESH,
            )

        def loop(self, count, step):
            def one(k, carry):
                step(k)
                return carry

            lax.fori_loop(1, count, one, 0)

        def first(self):
            self.loop(nn, lambda k: self.near(k).start())

        def second(self):
            self.loop(nn, lambda k: self.near(k).wait())
            self.loop(nw, lambda k: self.far(k).start())

        def finish(self):
            self.loop(nw, lambda k: self.far(k).wait())

    for edge, side in ((iw == 0, 0), (iw == nw - 1, 1)):
        @pl.when(edge)
        def _():
            blank = jnp.zeros((by, bz), f32)
            chx[side] = blank
            for turn in range(3):
                pqr[turn, side] = blank
                yr[turn, side] = blank
            for turn in range(2):
                hx[turn, side] = blank

    for edge, side in ((inn == 0, 0), (inn == nn - 1, 1)):
        @pl.when(edge)
        def _():
            blank = jnp.zeros((bx, bz), f32)
            chy[side] = blank
            for turn in range(2):
                hy[turn, side] = blank

    cys[0] = con[:, 0, :]
    cys[1] = con[:, by - 1, :]
    cond_x = pair(con.at[0], con.at[bx - 1], chx, 0, "wide")
    cond_y = pair(cys.at[0], cys.at[1], chy, 2, "narrow")
    def fold8(value):
        return value.reshape(value.shape[0] // 8, 8, bz).sum(axis=0)

    half_y, half_x = by // 2, bx // 2
    zero8 = jnp.zeros((8, bz), f32)

    def post(ref, rows):
        for k, row in enumerate(rows):
            ref[iw, inn, pl.ds(k, 1), :] = jnp.sum(row, axis=0, keepdims=True)

    def means_of(field):
        rows = []
        for part in range(2):
            def one(x, carry):
                value = field[x]
                return carry[0] + fold8(value[:half_y]), carry[1] + fold8(value[half_y:])

            rows += list(lax.fori_loop(part * half_x, (part + 1) * half_x, one, (zero8, zero8)))
        return rows

    gather_a, gather_b, gather_c, gather_d = (
        Gather(ref, slot) for slot, ref in enumerate((ga, gb, gc, gd))
    )
    post(ga, means_of(src) + [zero8] * 4)

    def along_z(value):
        high, low = split(value)
        both = jnp.dot(
            jnp.concatenate([high, low], axis=1), tabz[...], preferred_element_type=f32
        )
        return both[:, :bz] + both[:, bz:]

    def along_y(value):
        high, low = split(value)
        pairs = jnp.concatenate([high, low], axis=1)
        both = jnp.dot(
            taby[...], jnp.concatenate([pairs, pairs], axis=0), preferred_element_type=f32
        )
        return both[:, :bz] + both[:, bz:]

    step = bx

    def forward(field, out):
        def one(k, carry):
            rows = pl.ds(k * step, step)
            value = along_z(field[rows].reshape(step * by, bz))
            for j in range(step):
                out[k * step + j] = along_y(value[j * by : (j + 1) * by])
            return carry

        lax.fori_loop(0, bx // step, one, 0)

    chunk = by // 2
    on_left = (iw > 0).astype(f32)
    on_right = (iw < nw - 1).astype(f32)

    def chunks(work):
        def one(k, carry):
            work(pl.ds(pl.multiple_of(k * chunk, chunk), chunk))
            return carry

        lax.fori_loop(0, by // chunk, one, 0)

    def eliminate(rows):
        diagonal = 2.0 + SHIFT + eigy[rows, :] + eigz[...]
        last = 1.0 / diagonal
        cp[0, rows, :] = last
        for k in range(1, W + bx):
            last = 1.0 / (diagonal - last)
            cp[k, rows, :] = last
        inv[rows, :] = 1.0 / (1.0 - last * cp[W - 1, rows, :])

    chunks(eliminate)

    def solve(turn, spec, out):
        def ends(rows):
            value = jnp.zeros((chunk, bz), f32)
            for k in range(W):
                value = (spec[bx - W + k, rows, :] + value) * cp[k, rows, :]
                tail[k, rows, :] = value
            pqs[turn, 1, rows, :] = value
            value = jnp.zeros((chunk, bz), f32)
            for t in reversed(range(W)):
                value = (spec[t, rows, :] + value) * cp[W - 1 - t, rows, :]
                head[t, rows, :] = value
            pqs[turn, 0, rows, :] = value

        chunks(ends)
        rims = pair(pqs.at[turn, 0], pqs.at[turn, 1], pqr.at[turn], 4 + 4 * turn, "wide")
        each(rims, "start")
        yield
        each(rims, "arrive")

        def middle(rows):
            value = pqr[turn, 0, rows, :]
            for t in range(bx):
                value = (spec[t, rows, :] + value) * cp[W + t, rows, :]
                if t < bx - 1:
                    own[t, rows, :] = value
            value = (value + cp[W + bx - 1, rows, :] * pqr[turn, 1, rows, :]) * inv[rows, :]
            own[bx - 1, rows, :] = value
            for t in reversed(range(bx - 1)):
                value = own[t, rows, :] + cp[W + t, rows, :] * value
                own[t, rows, :] = value

        chunks(middle)
        backs = pair(own.at[0], own.at[bx - 1], yr.at[turn], 6 + 4 * turn, "wide")
        each(backs, "start")
        yield
        each(backs, "arrive")

        def fold(rows):
            value = yr[turn, 1, rows, :]
            for k in reversed(range(W)):
                value = tail[k, rows, :] + cp[k, rows, :] * value
                t = bx - W + k
                out[t, rows, :] = own[t, rows, :] + on_right * value
            value = yr[turn, 0, rows, :]
            for t in range(W):
                value = head[t, rows, :] + cp[W - 1 - t, rows, :] * value
                out[t, rows, :] = own[t, rows, :] + on_left * value

        chunks(fold)
        each(rims, "leave")
        each(backs, "leave")
        yield

    lanes = lax.broadcasted_iota(jnp.int32, (1, bz), 1)

    def inverse(correction, out, combine):
        spread = []
        for o in range(0, PRIMAL, 2):
            row = jnp.where(lanes < bz // 2, correction[o], correction[o + 1])
            spread.append(jnp.broadcast_to(row, (half_y, bz)))
        spread = [jnp.concatenate(spread[o : o + 2], axis=0) for o in (0, 2)]
        value = along_z(jnp.concatenate([along_y(combine(x)) for x in range(bx)], axis=0))
        for x in range(bx):
            out[x] = value[x * by : (x + 1) * by] + spread[x // half_x]

    scale = 1.0 / (half_x * half_y * (bz // 2))

    def correct(ref):
        both = jnp.dot(
            wide_rows[...], ref[...].reshape(nw * nn * 8, bz),
            precision=lax.Precision.HIGHEST, preferred_element_type=f32,
        )
        upper = lax.broadcasted_iota(jnp.int32, (2 * PRIMAL, bz), 1) >= bz // 2
        second = lax.broadcasted_iota(jnp.int32, (2 * PRIMAL, bz), 0) >= PRIMAL
        both = jnp.sum(jnp.where(upper == second, both, 0.0), axis=1, keepdims=True)
        both = (both[:PRIMAL] + both[PRIMAL:]) * scale
        return [both[o : o + 1] for o in range(PRIMAL)]

    def lay_out():
        block = 128
        entry = lax.broadcasted_iota(jnp.int32, (block, block), 0)
        place_of = lax.broadcasted_iota(jnp.int32, (block, block), 1)
        device, row = place_of // 8, place_of % 8
        for side in range(2):
            chosen = jnp.where((row < 4) & (entry == device * 8 + 2 * row + side), 1.0, 0.0)
            for k in range(nw * nn * 8 // block):
                columns = slice(k * block, (k + 1) * block)
                wide_rows[side * PRIMAL : (side + 1) * PRIMAL, columns] = jnp.dot(
                    cinv[0, 0, :, columns], chosen.astype(f32),
                    precision=lax.Precision.HIGHEST, preferred_element_type=f32,
                )

    lay_out()

    def dots(ref):
        whole = jnp.sum(ref[...].reshape(nw * nn, 8, bz), axis=0)
        return [jnp.sum(whole[k : k + 1], axis=1, keepdims=True) for k in range(4, 7)]

    index_y = lax.broadcasted_iota(jnp.int32, (by, bz), 0)

    def weights():
        each(cond_x + cond_y, "arrive")
        index_z = lax.broadcasted_iota(jnp.int32, (by, bz), 1)
        fx[0] = harmonic(chx[0], con[0])
        fx[bx] = harmonic(con[bx - 1], chx[1])

        def one(x, carry):
            value = con[x]
            fy[x] = jnp.where(
                index_y == by - 1, 0.0, harmonic(value, pltpu.roll(value, by - 1, 0))
            )
            fz[x] = jnp.where(
                index_z == bz - 1, 0.0, harmonic(value, pltpu.roll(value, bz - 1, 1))
            )
            return carry

        def between(x, carry):
            fx[x] = harmonic(con[x - 1], con[x])
            return carry

        lax.fori_loop(0, bx, one, 0)
        lax.fori_loop(1, bx, between, 0)
        fylo[...] = harmonic(cys[0], chy[0])
        fyhi[...] = harmonic(cys[1], chy[1])
        each(cond_x + cond_y, "leave")

    def apply(turn, field, out, inner):
        hys[turn, 0] = field[:, 0, :]
        hys[turn, 1] = field[:, by - 1, :]
        slot = 16 + 4 * turn
        layers = pair(field.at[0], field.at[bx - 1], hx.at[turn], slot, "wide") + pair(
            hys.at[turn, 0], hys.at[turn, 1], hy.at[turn], slot + 2, "narrow"
        )
        each(layers, "start")

        def point(x, below, above):
            value = field[x]
            result = rea[x] * value
            result = result + fx[x + 1] * (value - above) + fx[x] * (value - below)
            flux = fy[x] * (value - pltpu.roll(value, by - 1, 0))
            result = result + flux - pltpu.roll(flux, 1, 0)
            flux = fz[x] * (value - pltpu.roll(value, bz - 1, 1))
            result = result + flux - pltpu.roll(flux, 1, 1)
            out[x] = result
            return value, result

        def gather_up(x, below, above, carry):
            value, result = point(x, below, above)
            extra = inner(x, value, result)
            return (
                carry[0] + fold8(result[:half_y]), carry[1] + fold8(result[half_y:]),
            ) + tuple(c + fold8(e) for c, e in zip(carry[2:], extra))

        parts = []
        products = (zero8,) * 3
        for low, high in ((1, half_x), (half_x, bx - 1)):
            carry = lax.fori_loop(
                low, high, lambda x, c: gather_up(x, field[x - 1], field[x + 1], c),
                (zero8, zero8) + products, unroll=True,
            )
            parts.append(carry[:2])
            products = carry[2:]
        each(layers, "arrive")
        carry = gather_up(0, hx[turn, 0], field[1], parts[0] + products)
        parts[0] = carry[:2]
        carry = gather_up(bx - 1, field[bx - 2], hx[turn, 1], parts[1] + carry[2:])
        parts[1] = carry[:2]
        products = list(carry[2:])
        low = fylo[...] * (hys[turn, 0] - hy[turn, 0])
        high = fyhi[...] * (hys[turn, 1] - hy[turn, 1])
        out[:, 0, :] = out[:, 0, :] + low
        out[:, by - 1, :] = out[:, by - 1, :] + high
        products[1] = products[1] + fold8(hys[turn, 0] * low + hys[turn, 1] * high)
        sums = []
        for part in range(2):
            planes = slice(part * half_x, (part + 1) * half_x)
            sums += [
                parts[part][0] + fold8(low[planes]), parts[part][1] + fold8(high[planes]),
            ]
        each(layers, "leave")
        return sums + products + [zero8]

    def local(turn, field, out, gather, between):
        stages = solve(turn, field, out)
        next(stages)
        gather.second()
        next(stages)
        between()
        next(stages)
        gather.finish()

    forward(src, spec)
    pl.semaphore_wait(barrier, nw + nn - 2)
    each(cond_x + cond_y, "start")
    gather_a.first()
    local(0, spec, total, gather_a, weights)
    coarse = correct(ga)
    inverse(coarse, z0, lambda x: total[x])
    post(gb, apply(0, z0, w0, lambda x, v, a: (src[x] * v, v * a, zero8)))
    gather_b.first()

    forward(w0, spec0)
    local(1, spec0, total0, gather_b, lambda: None)
    gamma0, delta0, _ = dots(gb)
    alpha0 = gamma0 / delta0
    coarse_b = correct(gb)
    coarse = [a - alpha0 * b for a, b in zip(coarse, coarse_b)]

    def first_step(x):
        value = total[x] - alpha0 * total0[x]
        total[x] = value
        return value

    inverse(coarse, z1, first_step)

    def inner(x, value, result):
        image = w0[x]
        return (src[x] - alpha0 * image) * value, value * result, value * image

    post(gc, apply(1, z1, w1, inner))
    gather_c.first()

    forward(w1, spec1)
    local(2, spec1, total1, gather_c, lambda: None)
    gamma1, own1, cross1 = dots(gc)
    beta1 = gamma1 / gamma0
    alpha1 = gamma1 / (own1 + 2.0 * beta1 * cross1 + beta1 * beta1 * delta0)

    def results():
        def one(x, carry):
            direction = z1[x] + beta1 * z0[x]
            x_out[x] = alpha0 * z0[x] + alpha1 * direction
            image = w0[x]
            r_out[x] = (src[x] - alpha0 * image) - alpha1 * (w1[x] + beta1 * image)
            z1[x] = direction
            return carry

        lax.fori_loop(0, bx, one, 0, unroll=4)

    coarse_c = correct(gc)
    coarse = [a - alpha1 * (c + beta1 * b) for a, b, c in zip(coarse, coarse_b, coarse_c)]

    def last_product(x, carry):
        value = total[x] - alpha1 * (total1[x] + beta1 * total0[x])
        total[x] = value
        image = spec0[x]
        remaining = (spec[x] - alpha0 * image) - alpha1 * (spec1[x] + beta1 * image)
        return carry + fold8(remaining * value)

    product = lax.fori_loop(0, bx, last_product, zero8, unroll=4)
    image_sums = gb[iw, inn]
    residual_sums = (ga[iw, inn] - alpha0 * image_sums) - alpha1 * (
        gc[iw, inn] + beta1 * image_sums
    )
    coarse_product = jnp.zeros((1, bz), f32)
    for o in range(0, PRIMAL, 2):
        row = jnp.where(lanes < bz // 2, coarse[o], coarse[o + 1])
        coarse_product = coarse_product + residual_sums[o // 2 : o // 2 + 1] * row
    post(gd, [zero8] * 4 + [product, coarse_product] + [zero8] * 2)
    gather_d.first()
    results()
    gather_d.second()
    inverse(coarse, d_out, lambda x: total[x])
    gather_d.finish()
    parts = dots(gd)
    beta2 = (parts[0] + parts[1]) / gamma1

    def last(x, carry):
        d_out[x] = d_out[x] + beta2 * z1[x]
        return carry

    lax.fori_loop(0, bx, last, 0, unroll=4)


def body(nw, nn, source, reaction, conductance, coarse_inverse):
    bx, by, bz = source.shape
    table_y, eigen_y = sine_basis(by)
    table_z, eigen_z = sine_basis(bz)

    def parts(table):
        table = np.asarray(table, np.float32)
        high = table.astype(jnp.bfloat16)
        low = (table - high.astype(np.float32)).astype(jnp.bfloat16)
        return np.concatenate([high, low], axis=1)

    tab_y = parts(table_y)
    tab_z = parts(table_z)
    tab_z = np.concatenate([tab_z, tab_z], axis=0)
    block = (bx, by, bz)
    layer = (by, bz)

    def vm(*shape):
        return pltpu.VMEM(shape, f32)

    scratch = [
        vm(*block), vm(*block), vm(*block), vm(*block), vm(*block), vm(*block), vm(*block),
        vm(W, *layer), vm(W, *layer), vm(W + bx, *layer), vm(*layer),
        vm(bx + 1, *layer), vm(*block), vm(bx, bz), vm(bx, bz), vm(*block),
        vm(*block), vm(*block), vm(*block), vm(*block),
        vm(2, *layer), vm(2, bx, bz), vm(2, bx, bz),
        vm(3, 2, *layer), vm(3, 2, *layer), vm(3, 2, *layer),
        vm(2, 2, *layer), vm(2, 2, bx, bz), vm(2, 2, bx, bz),
        vm(nw, nn, 8, bz), vm(nw, nn, 8, bz), vm(nw, nn, 8, bz), vm(nw, nn, 8, bz),
        vm(2 * PRIMAL, nw * nn * 8),
        pltpu.SemaphoreType.DMA((24,)), pltpu.SemaphoreType.DMA((24,)),
        pltpu.SemaphoreType.DMA((4, nn)), pltpu.SemaphoreType.DMA((4, nn)),
        pltpu.SemaphoreType.DMA((4, nw)), pltpu.SemaphoreType.DMA((4, nw)),
    ]
    spec = pl.BlockSpec(memory_space=pltpu.VMEM)
    return pl.pallas_call(
        functools.partial(kernel, nw, nn),
        out_shape=[jax.ShapeDtypeStruct(block, f32)] * 3,
        in_specs=[spec] * 8,
        out_specs=[spec] * 3,
        scratch_shapes=scratch,
        compiler_params=pltpu.CompilerParams(
            collective_id=0, has_side_effects=True, vmem_limit_bytes=32 * 1024 * 1024
        ),
    )(
        source, reaction, conductance, coarse_inverse,
        jnp.asarray(tab_z), jnp.asarray(tab_y),
        jnp.asarray(eigen_y.reshape(-1, 1), f32), jnp.asarray(eigen_z.reshape(1, -1), f32),
    )


def solution(mesh):
    grid = P("wide", "narrow", None)
    return jax.shard_map(
        functools.partial(body, mesh.shape["wide"], mesh.shape["narrow"]),
        mesh=mesh,
        in_specs=(grid, grid, grid, P("wide", "narrow", None, None)),
        out_specs=(grid, grid, grid),
        check_vma=False,
    )
```

```python
import functools

import jax
import jax.numpy as jnp
import numpy as np
from jax import lax
from jax.experimental import pallas as pl
from jax.experimental.pallas import tpu as pltpu
from jax.sharding import PartitionSpec as P

W = 8
PRIMAL = 8
SHIFT = 0.06
MESH = pl.DeviceIdType.MESH
f32 = jnp.float32
bf16 = jnp.bfloat16


def sine_basis(extent):
    indices = np.arange(extent, dtype=np.float64) + 1.0
    angles = np.pi * indices[:, None] * indices[None, :] / (extent + 1)
    table = np.sqrt(2.0 / (extent + 1)) * np.sin(angles)
    eigen = 2.0 - 2.0 * np.cos(np.pi * indices / (extent + 1))
    return table, eigen


def split(value):
    high = value.astype(bf16)
    return high, (value - high.astype(f32)).astype(bf16)


def harmonic(first, second):
    return 2.0 * first * second / (first + second)


def kernel(
    nw, nn, src, rea, con, cinv, tabz, taby, eigy, eigz, x_out, r_out, d_out,
    spec, spec0, spec1, own, total, total0, total1, tail, head, cp, inv, fx, fy, fylo, fyhi, fz,
    z0, z1, w0, w1, chx, chy, cys, pqs, pqr, yr, hx, hy, hys, ga, gb, gc, gd,
    wide_rows, nsend, nrecv, gs1, gr1, gs2, gr2,
):
    bx, by, bz = src.shape
    iw, inn = lax.axis_index("wide"), lax.axis_index("narrow")
    place = {"wide": (iw, nw), "narrow": (inn, nn)}

    barrier = pltpu.get_barrier_semaphore()

    def greet(axis):
        me, count = place[axis]

        def one(k, carry):
            pl.semaphore_signal(
                barrier, inc=1, device_id={axis: lax.rem(me + k, count)}, device_id_type=MESH
            )
            return carry

        lax.fori_loop(1, count, one, 0)

    greet("wide")
    greet("narrow")

    class Shift:
        def __init__(self, source, target, slot, axis, step):
            me, count = place[axis]
            if step > 0:
                self.sends, self.gets = me < count - 1, me > 0
            else:
                self.sends, self.gets = me > 0, me < count - 1
            self.copy = pltpu.make_async_remote_copy(
                src_ref=source, dst_ref=target, send_sem=nsend.at[slot], recv_sem=nrecv.at[slot],
                device_id={axis: me + step}, device_id_type=MESH,
            )

        def start(self):
            @pl.when(self.sends)
            def _():
                self.copy.start()

        def arrive(self):
            @pl.when(self.gets)
            def _():
                self.copy.wait_recv()

        def leave(self):
            @pl.when(self.sends)
            def _():
                self.copy.wait_send()

    def pair(low_source, high_source, target, slot, axis):
        return (
            Shift(high_source, target.at[0], slot, axis, 1),
            Shift(low_source, target.at[1], slot + 1, axis, -1),
        )

    def each(copies, verb):
        for copy in copies:
            getattr(copy, verb)()

    class Gather:
        def __init__(self, ref, slot):
            self.ref, self.slot = ref, slot

        def near(self, k):
            return pltpu.make_async_remote_copy(
                src_ref=self.ref.at[iw, inn], dst_ref=self.ref.at[iw, inn],
                send_sem=gs1.at[self.slot, k], recv_sem=gr1.at[self.slot, k],
                device_id={"narrow": lax.rem(inn + k, nn)}, device_id_type=MESH,
            )

        def far(self, k):
            return pltpu.make_async_remote_copy(
                src_ref=self.ref.at[iw], dst_ref=self.ref.at[iw],
                send_sem=gs2.at[self.slot, k], recv_sem=gr2.at[self.slot, k],
                device_id={"wide": lax.rem(iw + k, nw)}, device_id_type=MESH,
            )

        def loop(self, count, step):
            def one(k, carry):
                step(k)
                return carry

            lax.fori_loop(1, count, one, 0)

        def first(self):
            self.loop(nn, lambda k: self.near(k).start())

        def second(self):
            self.loop(nn, lambda k: self.near(k).wait())
            self.loop(nw, lambda k: self.far(k).start())

        def finish(self):
            self.loop(nw, lambda k: self.far(k).wait())

    for edge, side in ((iw == 0, 0), (iw == nw - 1, 1)):
        @pl.when(edge)
        def _():
            blank = jnp.zeros((by, bz), f32)
            chx[side] = blank
            for turn in range(3):
                pqr[turn, side] = blank
                yr[turn, side] = blank
            for turn in range(2):
                hx[turn, side] = blank

    for edge, side in ((inn == 0, 0), (inn == nn - 1, 1)):
        @pl.when(edge)
        def _():
            blank = jnp.zeros((bx, bz), f32)
            chy[side] = blank
            for turn in range(2):
                hy[turn, side] = blank

    cys[0] = con[:, 0, :]
    cys[1] = con[:, by - 1, :]
    cond_x = pair(con.at[0], con.at[bx - 1], chx, 0, "wide")
    cond_y = pair(cys.at[0], cys.at[1], chy, 2, "narrow")
    def fold8(value):
        return value.reshape(value.shape[0] // 8, 8, bz).sum(axis=0)

    half_y, half_x = by // 2, bx // 2
    zero8 = jnp.zeros((8, bz), f32)

    def post(ref, rows):
        for k, row in enumerate(rows):
            ref[iw, inn, pl.ds(k, 1), :] = jnp.sum(row, axis=0, keepdims=True)

    def means_of(field):
        rows = []
        for part in range(2):
            def one(x, carry):
                value = field[x]
                return carry[0] + fold8(value[:half_y]), carry[1] + fold8(value[half_y:])

            rows += list(lax.fori_loop(part * half_x, (part + 1) * half_x, one, (zero8, zero8)))
        return rows

    gather_a, gather_b, gather_c, gather_d = (
        Gather(ref, slot) for slot, ref in enumerate((ga, gb, gc, gd))
    )
    post(ga, means_of(src) + [zero8] * 4)

    def along_z(value):
        high, low = split(value)
        both = jnp.dot(
            jnp.concatenate([high, low], axis=1), tabz[...], preferred_element_type=f32
        )
        return both[:, :bz] + both[:, bz:]

    def along_y(value):
        high, low = split(value)
        pairs = jnp.concatenate([high, low], axis=1)
        both = jnp.dot(
            taby[...], jnp.concatenate([pairs, pairs], axis=0), preferred_element_type=f32
        )
        return both[:, :bz] + both[:, bz:]

    step = bx

    def forward(field, out):
        def one(k, carry):
            rows = pl.ds(k * step, step)
            value = along_z(field[rows].reshape(step * by, bz))
            for j in range(step):
                out[k * step + j] = along_y(value[j * by : (j + 1) * by])
            return carry

        lax.fori_loop(0, bx // step, one, 0)

    chunk = by // 2
    on_left = (iw > 0).astype(f32)
    on_right = (iw < nw - 1).astype(f32)

    def chunks(work):
        def one(k, carry):
            work(pl.ds(pl.multiple_of(k * chunk, chunk), chunk))
            return carry

        lax.fori_loop(0, by // chunk, one, 0)

    def eliminate(rows):
        diagonal = 2.0 + SHIFT + eigy[rows, :] + eigz[...]
        last = 1.0 / diagonal
        cp[0, rows, :] = last
        for k in range(1, W + bx):
            last = 1.0 / (diagonal - last)
            cp[k, rows, :] = last
        inv[rows, :] = 1.0 / (1.0 - last * cp[W - 1, rows, :])

    chunks(eliminate)

    def solve(turn, spec, out):
        def ends(rows):
            value = jnp.zeros((chunk, bz), f32)
            for k in range(W):
                value = (spec[bx - W + k, rows, :] + value) * cp[k, rows, :]
                tail[k, rows, :] = value
            pqs[turn, 1, rows, :] = value
            value = jnp.zeros((chunk, bz), f32)
            for t in reversed(range(W)):
                value = (spec[t, rows, :] + value) * cp[W - 1 - t, rows, :]
                head[t, rows, :] = value
            pqs[turn, 0, rows, :] = value

        chunks(ends)
        rims = pair(pqs.at[turn, 0], pqs.at[turn, 1], pqr.at[turn], 4 + 4 * turn, "wide")
        each(rims, "start")
        yield
        each(rims, "arrive")

        def middle(rows):
            value = pqr[turn, 0, rows, :]
            for t in range(bx):
                value = (spec[t, rows, :] + value) * cp[W + t, rows, :]
                if t < bx - 1:
                    own[t, rows, :] = value
            value = (value + cp[W + bx - 1, rows, :] * pqr[turn, 1, rows, :]) * inv[rows, :]
            own[bx - 1, rows, :] = value
            for t in reversed(range(bx - 1)):
                value = own[t, rows, :] + cp[W + t, rows, :] * value
                own[t, rows, :] = value

        chunks(middle)
        backs = pair(own.at[0], own.at[bx - 1], yr.at[turn], 6 + 4 * turn, "wide")
        each(backs, "start")
        yield
        each(backs, "arrive")

        def fold(rows):
            value = yr[turn, 1, rows, :]
            for k in reversed(range(W)):
                value = tail[k, rows, :] + cp[k, rows, :] * value
                t = bx - W + k
                out[t, rows, :] = own[t, rows, :] + on_right * value
            value = yr[turn, 0, rows, :]
            for t in range(W):
                value = head[t, rows, :] + cp[W - 1 - t, rows, :] * value
                out[t, rows, :] = own[t, rows, :] + on_left * value

        chunks(fold)
        each(rims, "leave")
        each(backs, "leave")
        yield

    lanes = lax.broadcasted_iota(jnp.int32, (1, bz), 1)

    def inverse(correction, out, combine, turn=None):
        spread = []
        for o in range(0, PRIMAL, 2):
            row = jnp.where(lanes < bz // 2, correction[o], correction[o + 1])
            spread.append(jnp.broadcast_to(row, (half_y, bz)))
        spread = [jnp.concatenate(spread[o : o + 2], axis=0) for o in (0, 2)]

        def planes(rows):
            value = along_z(jnp.concatenate([along_y(combine(x)) for x in rows], axis=0))
            for k, x in enumerate(rows):
                out[x] = value[k * by : (k + 1) * by] + spread[x // half_x]

        if turn is None:
            planes(range(bx))
        else:
            planes([0, bx - 1])
            each(outer_planes(turn, out), "start")
            planes(range(1, bx - 1))

    def outer_planes(turn, field):
        return pair(field.at[0], field.at[bx - 1], hx.at[turn], 16 + 4 * turn, "wide")

    scale = 1.0 / (half_x * half_y * (bz // 2))

    def correct(ref):
        both = jnp.dot(
            wide_rows[...], ref[...].reshape(nw * nn * 8, bz),
            precision=lax.Precision.HIGHEST, preferred_element_type=f32,
        )
        upper = lax.broadcasted_iota(jnp.int32, (2 * PRIMAL, bz), 1) >= bz // 2
        second = lax.broadcasted_iota(jnp.int32, (2 * PRIMAL, bz), 0) >= PRIMAL
        both = jnp.sum(jnp.where(upper == second, both, 0.0), axis=1, keepdims=True)
        both = (both[:PRIMAL] + both[PRIMAL:]) * scale
        return [both[o : o + 1] for o in range(PRIMAL)]

    def lay_out():
        block = 128
        entry = lax.broadcasted_iota(jnp.int32, (block, block), 0)
        place_of = lax.broadcasted_iota(jnp.int32, (block, block), 1)
        device, row = place_of // 8, place_of % 8
        for side in range(2):
            chosen = jnp.where((row < 4) & (entry == device * 8 + 2 * row + side), 1.0, 0.0)
            for k in range(nw * nn * 8 // block):
                columns = slice(k * block, (k + 1) * block)
                wide_rows[side * PRIMAL : (side + 1) * PRIMAL, columns] = jnp.dot(
                    cinv[0, 0, :, columns], chosen.astype(f32),
                    precision=lax.Precision.HIGHEST, preferred_element_type=f32,
                )

    lay_out()

    def dots(ref):
        whole = jnp.sum(ref[...].reshape(nw * nn, 8, bz), axis=0)
        return [jnp.sum(whole[k : k + 1], axis=1, keepdims=True) for k in range(4, 7)]

    index_y = lax.broadcasted_iota(jnp.int32, (by, bz), 0)

    def weights():
        each(cond_x + cond_y, "arrive")
        index_z = lax.broadcasted_iota(jnp.int32, (by, bz), 1)
        fx[0] = harmonic(chx[0], con[0])
        fx[bx] = harmonic(con[bx - 1], chx[1])

        def one(x, carry):
            value = con[x]
            fy[x] = jnp.where(
                index_y == by - 1, 0.0, harmonic(value, pltpu.roll(value, by - 1, 0))
            )
            fz[x] = jnp.where(
                index_z == bz - 1, 0.0, harmonic(value, pltpu.roll(value, bz - 1, 1))
            )
            return carry

        def between(x, carry):
            fx[x] = harmonic(con[x - 1], con[x])
            return carry

        lax.fori_loop(0, bx, one, 0)
        lax.fori_loop(1, bx, between, 0)
        fylo[...] = harmonic(cys[0], chy[0])
        fyhi[...] = harmonic(cys[1], chy[1])
        each(cond_x + cond_y, "leave")

    def apply(turn, field, out, inner):
        hys[turn, 0] = field[:, 0, :]
        hys[turn, 1] = field[:, by - 1, :]
        slot = 16 + 4 * turn
        sides = pair(hys.at[turn, 0], hys.at[turn, 1], hy.at[turn], slot + 2, "narrow")
        each(sides, "start")
        layers = outer_planes(turn, field) + sides

        def point(x, below, above):
            value = field[x]
            result = rea[x] * value
            result = result + fx[x + 1] * (value - above) + fx[x] * (value - below)
            flux = fy[x] * (value - pltpu.roll(value, by - 1, 0))
            result = result + flux - pltpu.roll(flux, 1, 0)
            flux = fz[x] * (value - pltpu.roll(value, bz - 1, 1))
            result = result + flux - pltpu.roll(flux, 1, 1)
            out[x] = result
            return value, result

        def gather_up(x, below, above, carry):
            value, result = point(x, below, above)
            extra = inner(x, value, result)
            return (
                carry[0] + fold8(result[:half_y]), carry[1] + fold8(result[half_y:]),
            ) + tuple(c + fold8(e) for c, e in zip(carry[2:], extra))

        parts = []
        products = (zero8,) * 3
        for low, high in ((1, half_x), (half_x, bx - 1)):
            carry = lax.fori_loop(
                low, high, lambda x, c: gather_up(x, field[x - 1], field[x + 1], c),
                (zero8, zero8) + products, unroll=True,
            )
            parts.append(carry[:2])
            products = carry[2:]
        each(layers, "arrive")
        carry = gather_up(0, hx[turn, 0], field[1], parts[0] + products)
        parts[0] = carry[:2]
        carry = gather_up(bx - 1, field[bx - 2], hx[turn, 1], parts[1] + carry[2:])
        parts[1] = carry[:2]
        products = list(carry[2:])
        low = fylo[...] * (hys[turn, 0] - hy[turn, 0])
        high = fyhi[...] * (hys[turn, 1] - hy[turn, 1])
        out[:, 0, :] = out[:, 0, :] + low
        out[:, by - 1, :] = out[:, by - 1, :] + high
        products[1] = products[1] + fold8(hys[turn, 0] * low + hys[turn, 1] * high)
        sums = []
        for part in range(2):
            planes = slice(part * half_x, (part + 1) * half_x)
            sums += [
                parts[part][0] + fold8(low[planes]), parts[part][1] + fold8(high[planes]),
            ]
        each(layers, "leave")
        return sums + products + [zero8]

    def local(turn, field, out, gather, between):
        stages = solve(turn, field, out)
        next(stages)
        gather.second()
        next(stages)
        between()
        next(stages)
        gather.finish()

    forward(src, spec)
    pl.semaphore_wait(barrier, nw + nn - 2)
    each(cond_x + cond_y, "start")
    gather_a.first()
    local(0, spec, total, gather_a, weights)
    coarse = correct(ga)
    inverse(coarse, z0, lambda x: total[x], 0)
    post(gb, apply(0, z0, w0, lambda x, v, a: (src[x] * v, v * a, zero8)))
    gather_b.first()

    forward(w0, spec0)
    local(1, spec0, total0, gather_b, lambda: None)
    gamma0, delta0, _ = dots(gb)
    alpha0 = gamma0 / delta0
    coarse_b = correct(gb)
    coarse = [a - alpha0 * b for a, b in zip(coarse, coarse_b)]

    def first_step(x):
        value = total[x] - alpha0 * total0[x]
        total[x] = value
        return value

    inverse(coarse, z1, first_step, 1)

    def inner(x, value, result):
        image = w0[x]
        return (src[x] - alpha0 * image) * value, value * result, value * image

    post(gc, apply(1, z1, w1, inner))
    gather_c.first()

    forward(w1, spec1)
    local(2, spec1, total1, gather_c, lambda: None)
    gamma1, own1, cross1 = dots(gc)
    beta1 = gamma1 / gamma0
    alpha1 = gamma1 / (own1 + 2.0 * beta1 * cross1 + beta1 * beta1 * delta0)

    def results():
        def one(x, carry):
            direction = z1[x] + beta1 * z0[x]
            x_out[x] = alpha0 * z0[x] + alpha1 * direction
            image = w0[x]
            r_out[x] = (src[x] - alpha0 * image) - alpha1 * (w1[x] + beta1 * image)
            z1[x] = direction
            return carry

        lax.fori_loop(0, bx, one, 0, unroll=4)

    coarse_c = correct(gc)
    coarse = [a - alpha1 * (c + beta1 * b) for a, b, c in zip(coarse, coarse_b, coarse_c)]

    def last_product(x, carry):
        value = total[x] - alpha1 * (total1[x] + beta1 * total0[x])
        total[x] = value
        image = spec0[x]
        remaining = (spec[x] - alpha0 * image) - alpha1 * (spec1[x] + beta1 * image)
        return carry + fold8(remaining * value)

    product = lax.fori_loop(0, bx, last_product, zero8, unroll=4)
    image_sums = gb[iw, inn]
    residual_sums = (ga[iw, inn] - alpha0 * image_sums) - alpha1 * (
        gc[iw, inn] + beta1 * image_sums
    )
    coarse_product = jnp.zeros((1, bz), f32)
    for o in range(0, PRIMAL, 2):
        row = jnp.where(lanes < bz // 2, coarse[o], coarse[o + 1])
        coarse_product = coarse_product + residual_sums[o // 2 : o // 2 + 1] * row
    post(gd, [zero8] * 4 + [product, coarse_product] + [zero8] * 2)
    gather_d.first()
    results()
    gather_d.second()
    inverse(coarse, d_out, lambda x: total[x])
    gather_d.finish()
    parts = dots(gd)
    beta2 = (parts[0] + parts[1]) / gamma1

    def last(x, carry):
        d_out[x] = d_out[x] + beta2 * z1[x]
        return carry

    lax.fori_loop(0, bx, last, 0, unroll=4)


def body(nw, nn, source, reaction, conductance, coarse_inverse):
    bx, by, bz = source.shape
    table_y, eigen_y = sine_basis(by)
    table_z, eigen_z = sine_basis(bz)

    def parts(table):
        table = np.asarray(table, np.float32)
        high = table.astype(jnp.bfloat16)
        low = (table - high.astype(np.float32)).astype(jnp.bfloat16)
        return np.concatenate([high, low], axis=1)

    tab_y = parts(table_y)
    tab_z = parts(table_z)
    tab_z = np.concatenate([tab_z, tab_z], axis=0)
    block = (bx, by, bz)
    layer = (by, bz)

    def vm(*shape):
        return pltpu.VMEM(shape, f32)

    scratch = [
        vm(*block), vm(*block), vm(*block), vm(*block), vm(*block), vm(*block), vm(*block),
        vm(W, *layer), vm(W, *layer), vm(W + bx, *layer), vm(*layer),
        vm(bx + 1, *layer), vm(*block), vm(bx, bz), vm(bx, bz), vm(*block),
        vm(*block), vm(*block), vm(*block), vm(*block),
        vm(2, *layer), vm(2, bx, bz), vm(2, bx, bz),
        vm(3, 2, *layer), vm(3, 2, *layer), vm(3, 2, *layer),
        vm(2, 2, *layer), vm(2, 2, bx, bz), vm(2, 2, bx, bz),
        vm(nw, nn, 8, bz), vm(nw, nn, 8, bz), vm(nw, nn, 8, bz), vm(nw, nn, 8, bz),
        vm(2 * PRIMAL, nw * nn * 8),
        pltpu.SemaphoreType.DMA((24,)), pltpu.SemaphoreType.DMA((24,)),
        pltpu.SemaphoreType.DMA((4, nn)), pltpu.SemaphoreType.DMA((4, nn)),
        pltpu.SemaphoreType.DMA((4, nw)), pltpu.SemaphoreType.DMA((4, nw)),
    ]
    spec = pl.BlockSpec(memory_space=pltpu.VMEM)
    return pl.pallas_call(
        functools.partial(kernel, nw, nn),
        out_shape=[jax.ShapeDtypeStruct(block, f32)] * 3,
        in_specs=[spec] * 8,
        out_specs=[spec] * 3,
        scratch_shapes=scratch,
        compiler_params=pltpu.CompilerParams(
            collective_id=0, has_side_effects=True, vmem_limit_bytes=32 * 1024 * 1024
        ),
    )(
        source, reaction, conductance, coarse_inverse,
        jnp.asarray(tab_z), jnp.asarray(tab_y),
        jnp.asarray(eigen_y.reshape(-1, 1), f32), jnp.asarray(eigen_z.reshape(1, -1), f32),
    )


def solution(mesh):
    grid = P("wide", "narrow", None)
    return jax.shard_map(
        functools.partial(body, mesh.shape["wide"], mesh.shape["narrow"]),
        mesh=mesh,
        in_specs=(grid, grid, grid, P("wide", "narrow", None, None)),
        out_specs=(grid, grid, grid),
        check_vma=False,
    )
```
